256 devices in a mesh: dp: 16 (over z, x_hi), tensor: 16 (over y, x_lo, core).
Axes of the slice: x: 4 (x_hi: 2, x_lo: 2; x = x_hi * 2 + x_lo), y: 4, z: 8, core: 2. Of those that a mesh axis runs over, the one named last changes fastest.
Arguments:
- patches: bfloat16 [512, 256, 6144], P('dp', None, 'tensor'), may hold values from -6 to 6
- visible: int32 [512, 64], P('dp'), may hold values from 0 to 255, as said below
- block_perm: int32 [64], replicated, may hold values from 0 to 63, each once
- first_left: bfloat16 [64, 96, 96], P('tensor', 'dp'), may hold values from -0.625 to 0.625
- first_right: bfloat16 [96, 64, 256], P('tensor', 'dp'), may hold values from -0.75 to 0.75
- second_right: bfloat16 [96, 256, 64], P('tensor', 'dp'), may hold values from -0.375 to 0.375
- second_left: bfloat16 [64, 96, 96], P('tensor', 'dp'), may hold values from -0.625 to 0.625
- cotangent: bfloat16 [32768, 6144], P('dp', 'tensor'), may hold values from -6 to 6
Outputs:
- mlp_out: bfloat16 [32768, 6144], P('dp', 'tensor')
- token_grad: bfloat16 [32768, 6144], P('dp', 'tensor')
- grad_first_left: float32 [64, 96, 96], P('tensor', 'dp')
- grad_first_right: float32 [96, 64, 256], P('tensor', 'dp')
- grad_second_right: float32 [96, 256, 64], P('tensor', 'dp')
- grad_second_left: float32 [64, 96, 96], P('tensor', 'dp')
The draws below stay inside these ranges and needn't reach their ends.
Inputs may be any that keep to these rules, and one draw needn't show every extreme that they name: `visible`: each row holds 64 different patch indices in increasing order. `block_perm`: each block number appears once.
All inputs are finite; a program needn't handle non-finite values.
Results may differ from the reference program's by a relative error of at most 0.022.
Values may be sent and summed in bfloat16 or wider, within the bound.
No kernel may reach another device: no remote copies, remote signals or barrier semaphores. Data moves between devices by JAX's collectives and lax.ppermute only.
A program may use at most 128 MiB of HBM per device.

```python
import math
import jax
import jax.numpy as jnp
from jax import lax

NB = 64
BS = 96
HB = 256
NP = 256
VIS = 64
D = 6144
TOK_DEV = 2048
IMGS = 512
TOKENS = 32768
N_DP = 16


def draw_visible(key, part):
    key = jax.random.fold_in(key, 7)
    scores = jax.random.randint(key, (IMGS, NP), 0, 1 << 20, dtype=jnp.int32) * NP + jnp.arange(NP, dtype=jnp.int32)[None, :]
    scores = scores.at[0, 0].set(-2).at[0, NP - 1].set(-1)
    chosen = jnp.argsort(scores, axis=1, stable=True)[:, :VIS]
    return jnp.sort(chosen, axis=1).astype(jnp.int32)


def block_levels(own_key, extent, cuts, low, top_value):
    level, own = 1.0, jax.random.fold_in(own_key, 6)
    for dim, shards_of in cuts:
        steps = jnp.exp(jax.random.uniform(jax.random.fold_in(own, dim), (shards_of,), jnp.float32, low / len(cuts), top_value / len(cuts)))
        level = level * jnp.repeat(steps, extent[dim] // shards_of).reshape([-1 if axis == dim else 1 for axis in range(len(extent))])
    return level


def normal_values(rng, shape, scale, most, split=(), held_as=jnp.bfloat16):
    gain = block_levels(rng, shape, split, -0.22, 0.18) if split else 1.0
    drawn = jax.random.normal(rng, shape, jnp.float32) * scale * gain
    return jnp.minimum(jnp.maximum(drawn, -most), most).astype(held_as)


def setup_inputs(seed: int = 0) -> dict:
    seeds = jax.random.split(jax.random.key(seed), 9)
    return {
        "patches": normal_values(seeds[0], (IMGS, NP, D), 1.0, 6.0, ((0, 16), (2, 16))),
        "visible": draw_visible(jax.random.fold_in(seeds[8], 71), 0),
        "block_perm": jax.random.permutation(seeds[2], NB).astype(jnp.int32),
        "first_left": normal_values(seeds[3], (NB, BS, BS), BS ** -0.5, 0.625, ((0, 16), (1, 16))),
        "first_right": normal_values(seeds[4], (BS, NB, HB), NB ** -0.5, 0.75, ((0, 16), (1, 16))),
        "second_right": normal_values(seeds[5], (BS, HB, NB), HB ** -0.5, 0.375, ((0, 16), (1, 16))),
        "second_left": normal_values(seeds[6], (NB, BS, BS), BS ** -0.5, 0.625, ((0, 16), (1, 16))),
        "cotangent": normal_values(seeds[7], (TOKENS, D), 1.0, 6.0, ((0, 16), (1, 16))),
    }


root_ratio = math.sqrt(2.0 / math.pi)

def gelu_value(hidden):
    inner = root_ratio * (hidden + 0.044715 * hidden * hidden * hidden)
    return 0.5 * hidden * (1.0 + jnp.tanh(inner))

def gelu_slope(hidden):
    inner = root_ratio * (hidden + 0.044715 * hidden * hidden * hidden)
    tangent = jnp.tanh(inner)
    return 0.5 * (1.0 + tangent) + 0.5 * hidden * (1.0 - tangent * tangent) * root_ratio * (1.0 + 3.0 * 0.044715 * hidden * hidden)

def reference(patches, visible, block_perm, first_left, first_right, second_right, second_left, cotangent):
    picked = jnp.take_along_axis(patches, visible[:, :, None].astype(jnp.int32), axis=1)
    tokens_all = picked.reshape(N_DP, TOK_DEV, NB, BS)
    upstream_all = cotangent.reshape(N_DP, TOK_DEV, NB, BS)
    inverse = jnp.zeros((NB,), jnp.int32).at[block_perm].set(jnp.arange(NB, dtype=jnp.int32))
    left_one = first_left.astype(jnp.float32)
    right_one = first_right.astype(jnp.float32)
    right_two = second_right.astype(jnp.float32)
    left_two = second_left.astype(jnp.float32)

    def one_block(carry, item):
        tokens, upstream = item
        tokens_f = tokens.astype(jnp.float32)
        upstream_f = upstream.astype(jnp.float32)
        section_one = jnp.einsum('tbi,bij->tbj', tokens_f, left_one).astype(jnp.bfloat16)
        mixed_in = jnp.take(section_one, block_perm, axis=1)
        hidden = jnp.einsum('tcp,pck->tpk', mixed_in.astype(jnp.float32), right_one)
        activated = gelu_value(hidden).astype(jnp.bfloat16)
        mixed_out = jnp.einsum('tpk,pkc->tcp', activated.astype(jnp.float32), right_two).astype(jnp.bfloat16)
        returned = jnp.take(mixed_out, inverse, axis=1)
        output = jnp.einsum('tbi,bij->tbj', returned.astype(jnp.float32), left_two).astype(jnp.bfloat16)
        back_grad = jnp.einsum('tbj,bij->tbi', upstream_f, left_two).astype(jnp.bfloat16)
        grad_left_two = jnp.einsum('tbi,tbj->bij', returned.astype(jnp.float32), upstream_f)
        arrived_grad = jnp.take(back_grad, block_perm, axis=1).astype(jnp.float32)
        grad_act = jnp.einsum('tcp,pkc->tpk', arrived_grad, right_two)
        grad_right_two = jnp.einsum('tpk,tcp->pkc', activated.astype(jnp.float32), arrived_grad)
        grad_hidden = (grad_act * gelu_slope(hidden)).astype(jnp.bfloat16)
        grad_mixed = jnp.einsum('tpk,pck->tcp', grad_hidden.astype(jnp.float32), right_one).astype(jnp.bfloat16)
        grad_right_one = jnp.einsum('tcp,tpk->pck', mixed_in.astype(jnp.float32), grad_hidden.astype(jnp.float32))
        returned_grad = jnp.take(grad_mixed, inverse, axis=1).astype(jnp.float32)
        grad_left_one = jnp.einsum('tbi,tbj->bij', tokens_f, returned_grad)
        token_grad = jnp.einsum('tbj,bij->tbi', returned_grad, left_one).astype(jnp.bfloat16)
        carry = (carry[0] + grad_left_one, carry[1] + grad_right_one, carry[2] + grad_right_two, carry[3] + grad_left_two)
        return (carry, (output, token_grad))
    init = (jnp.zeros((NB, BS, BS), jnp.float32), jnp.zeros((BS, NB, HB), jnp.float32), jnp.zeros((BS, HB, NB), jnp.float32), jnp.zeros((NB, BS, BS), jnp.float32))
    totals, (outputs, token_grads) = lax.scan(one_block, init, (tokens_all, upstream_all))
    return (outputs.reshape(TOKENS, NB * BS), token_grads.reshape(TOKENS, NB * BS), totals[0], totals[1], totals[2], totals[3])
```

```python
import math

import jax
import jax.numpy as jnp
from jax import lax
from jax.experimental import pallas as pl
from jax.experimental.pallas import tpu as pltpu
from jax.sharding import PartitionSpec as P

BF16 = jnp.bfloat16
F32 = jnp.float32
NB, BS, HB = 64, 96, 256
POS = 6
LB = 4
FEAT = LB * BS
TOK = 2048
TILE = 512
STEPS = TOK // TILE
ROOT_RATIO = math.sqrt(2.0 / math.pi)
DP_ORDER = (8, 4, 2, 1)
PARAMS = pltpu.CompilerParams(vmem_limit_bytes=40 * 1024 * 1024)


def mm(lhs, rhs, left_dim=1, right_dim=0):
    return lax.dot_general(
        lhs, rhs, (((left_dim,), (right_dim,)), ((), ())), preferred_element_type=F32
    )


def whole(shape):
    return pl.BlockSpec(shape, lambda *_: (0,) * len(shape))


def columns(rows):
    return pl.BlockSpec((rows, TILE), lambda step: (0, step))


def token_rows():
    return pl.BlockSpec((TILE, FEAT), lambda step: (step, 0))


def struct(shape, dtype=BF16):
    return jax.ShapeDtypeStruct(shape, dtype)


def cost(flops, moved):
    return pl.CostEstimate(flops=flops, bytes_accessed=moved, transcendentals=0)


def pick_kernel(visible_ref, patches_ref, tokens_ref):
    images, patch_count, _ = patches_ref.shape
    vis = visible_ref.shape[2]
    for image in range(images):
        wanted = visible_ref[image]
        chosen = lax.broadcasted_iota(jnp.int32, (patch_count, vis), 0) == wanted
        rows = mm(chosen.astype(F32).astype(BF16), patches_ref[image], 0, 0)
        tokens_ref[image * vis : (image + 1) * vis, :] = rows.astype(BF16)


def pick(patches, visible):
    images, patch_count, feats = patches.shape
    vis = visible.shape[1]
    group = 8
    return pl.pallas_call(
        pick_kernel,
        grid=(images // group,),
        in_specs=[
            pl.BlockSpec((group, 1, vis), lambda step: (step, 0, 0)),
            pl.BlockSpec((group, patch_count, feats), lambda step: (step, 0, 0)),
        ],
        out_specs=pl.BlockSpec((group * vis, feats), lambda step: (step, 0)),
        out_shape=struct((images * vis, feats)),
        compiler_params=PARAMS,
        cost_estimate=cost(2 * TOK * patch_count * feats, 8 << 20),
        name="pick_patches",
    )(visible[:, None, :], patches)


def up_kernel(tokens_ref, pieces_ref, place_ref, rep_ref, mask_ref, matrix_ref, section_ref):
    @pl.when(pl.program_id(0) == 0)
    def _():
        flat = mm(pieces_ref[...], place_ref[...], 0, 0).astype(BF16)
        matrix_ref[...] = mm(rep_ref[...], flat).astype(BF16) * mask_ref[...]

    section_ref[...] = mm(matrix_ref[...], tokens_ref[...], 1, 1).astype(BF16)


def down_kernel(upstream_ref, pieces_ref, place_ref, tile_ref, mask_ref, matrix_ref, section_ref):
    @pl.when(pl.program_id(0) == 0)
    def _():
        tall = mm(place_ref[...], pieces_ref[...]).astype(BF16)
        matrix_ref[...] = mm(tall, tile_ref[...]).astype(BF16) * mask_ref[...]

    section_ref[...] = mm(matrix_ref[...], upstream_ref[...], 1, 1).astype(BF16)


def block_map(kernel, name, rows, pieces, place, spread, mask):
    return pl.pallas_call(
        kernel,
        grid=(STEPS,),
        in_specs=[
            token_rows(),
            whole(pieces.shape),
            whole(place.shape),
            whole(spread.shape),
            whole(mask.shape),
        ],
        out_specs=[whole((FEAT, FEAT)), columns(FEAT)],
        out_shape=[struct((FEAT, FEAT)), struct((FEAT, TOK))],
        compiler_params=PARAMS,
        cost_estimate=cost(2 * TOK * FEAT * FEAT * 3, 5 << 20),
        name=name,
    )(rows, pieces, place, spread, mask)


def forward_kernel(
    arrived_ref, perm_ref, right_one_ref, right_two_ref, mixed_ref, act_ref, slope_ref, leaving_ref, own_ref
):
    mixed_ref[...] = mm(perm_ref[...], arrived_ref[...]).astype(BF16)
    for pos in range(POS):
        rows = slice(pos * NB, (pos + 1) * NB)
        hidden_rows = slice(pos * HB, (pos + 1) * HB)
        hidden = mm(right_one_ref[pos], mixed_ref[rows, :], 0, 0)
        square = hidden * hidden
        tangent = jnp.tanh(hidden * (ROOT_RATIO + (ROOT_RATIO * 0.044715) * square))
        half = 0.5 * hidden
        act = (half + half * tangent).astype(BF16)
        slope = (0.5 + 0.5 * tangent) + half * (1.0 - tangent * tangent) * (
            ROOT_RATIO + (ROOT_RATIO * 3.0 * 0.044715) * square
        )
        act_ref[hidden_rows, :] = act
        slope_ref[hidden_rows, :] = slope.astype(BF16)
        own_ref[rows, :] = mm(right_two_ref[pos], act, 0, 0).astype(BF16)
    leaving_ref[...] = mm(perm_ref[...], own_ref[...], 0, 0).astype(BF16)


def mix_forward(arrived, perm, right_one, right_two):
    return pl.pallas_call(
        forward_kernel,
        grid=(STEPS,),
        in_specs=[
            columns(FEAT),
            whole((FEAT, FEAT)),
            whole((POS, NB, HB)),
            whole((POS, HB, NB)),
        ],
        out_specs=[columns(FEAT), columns(POS * HB), columns(POS * HB), columns(FEAT)],
        out_shape=[
            struct((FEAT, TOK)),
            struct((POS * HB, TOK)),
            struct((POS * HB, TOK)),
            struct((FEAT, TOK)),
        ],
        scratch_shapes=[pltpu.VMEM((FEAT, TILE), BF16)],
        compiler_params=PARAMS,
        cost_estimate=cost(12 * TOK * FEAT * FEAT, 17 << 20),
        name="mix_forward",
    )(arrived, perm, right_one, right_two)


def backward_kernel(
    arrived_ref,
    perm_ref,
    right_one_ref,
    right_two_ref,
    mixed_ref,
    act_ref,
    slope_ref,
    owner_ref,
    leaving_ref,
    grad_one_ref,
    grad_two_ref,
    grads_ref,
    own_ref,
    sum_one_ref,
    sum_two_ref,
):
    step = pl.program_id(0)

    @pl.when(step == 0)
    def _():
        sum_one_ref[...] = jnp.zeros_like(sum_one_ref)
        sum_two_ref[...] = jnp.zeros_like(sum_two_ref)

    grads_ref[...] = mm(perm_ref[...], arrived_ref[...]).astype(BF16)
    for pos in range(POS):
        rows = slice(pos * NB, (pos + 1) * NB)
        hidden_rows = slice(pos * HB, (pos + 1) * HB)
        grad_act = mm(right_two_ref[pos], grads_ref[rows, :])
        grad_hidden = (grad_act * slope_ref[hidden_rows, :].astype(F32)).astype(BF16)
        own_ref[rows, :] = mm(right_one_ref[pos], grad_hidden).astype(BF16)
        sum_one_ref[rows, :] += mm(mixed_ref[rows, :], grad_hidden, 1, 1)
        sum_two_ref[pos] += mm(act_ref[hidden_rows, :], grads_ref[rows, :], 1, 1)
    leaving_ref[...] = mm(perm_ref[...], own_ref[...], 0, 0).astype(BF16)

    @pl.when(step == STEPS - 1)
    def _():
        grad_one_ref[...] = mm(owner_ref[...], sum_one_ref[...].astype(BF16)).astype(BF16)
        for pos in range(POS // 2):
            pair = jnp.concatenate([sum_two_ref[pos], sum_two_ref[pos + POS // 2]], axis=1)
            pair = pair.astype(BF16)
            for owner in range(16):
                grad_two_ref[owner * 48 + pos * 16 : owner * 48 + pos * 16 + 16, :] = pair[
                    owner * 16 : owner * 16 + 16, :
                ]


def mix_backward(arrived, perm, right_one, right_two, mixed, act, slope, owner):
    return pl.pallas_call(
        backward_kernel,
        grid=(STEPS,),
        in_specs=[
            columns(FEAT),
            whole((FEAT, FEAT)),
            whole((POS, NB, HB)),
            whole((POS, HB, NB)),
            columns(FEAT),
            columns(POS * HB),
            columns(POS * HB),
            whole((FEAT, FEAT)),
        ],
        out_specs=[columns(FEAT), whole((FEAT, HB)), whole((768, 128))],
        out_shape=[struct((FEAT, TOK)), struct((FEAT, HB)), struct((768, 128))],
        scratch_shapes=[
            pltpu.VMEM((FEAT, TILE), BF16),
            pltpu.VMEM((FEAT, TILE), BF16),
            pltpu.VMEM((FEAT, HB), F32),
            pltpu.VMEM((POS, HB, NB), F32),
        ],
        compiler_params=PARAMS,
        cost_estimate=cost(20 * TOK * FEAT * FEAT, 17 << 20),
        name="mix_backward",
    )(arrived, perm, right_one, right_two, mixed, act, slope, owner)


def output_kernel(returned_ref, matrix_ref, upstream_ref, mask_ref, fold_ref, out_ref, grad_ref, sum_ref):
    step = pl.program_id(0)

    @pl.when(step == 0)
    def _():
        sum_ref[...] = jnp.zeros_like(sum_ref)

    out_ref[...] = mm(returned_ref[...], matrix_ref[...], 0, 0).astype(BF16)
    sum_ref[...] += mm(returned_ref[...], upstream_ref[...])

    @pl.when(step == STEPS - 1)
    def _():
        kept = sum_ref[...].astype(BF16) * mask_ref[...]
        grad_ref[...] = mm(kept, fold_ref[...]).astype(BF16)


def output_and_grad(returned, matrix, upstream, mask, fold):
    return pl.pallas_call(
        output_kernel,
        grid=(STEPS,),
        in_specs=[
            columns(FEAT),
            whole((FEAT, FEAT)),
            token_rows(),
            whole((FEAT, FEAT)),
            whole((FEAT, 128)),
        ],
        out_specs=[token_rows(), whole((FEAT, 128))],
        out_shape=[struct((TOK, FEAT)), struct((FEAT, 128))],
        scratch_shapes=[pltpu.VMEM((FEAT, FEAT), F32)],
        compiler_params=PARAMS,
        cost_estimate=cost(4 * TOK * FEAT * FEAT, 5 << 20),
        name="output_and_grad",
    )(returned, matrix, upstream, mask, fold)


def first_grad_kernel(returned_ref, tokens_ref, mask_ref, rep_ref, order_ref, grad_ref, sum_ref):
    step = pl.program_id(0)

    @pl.when(step == 0)
    def _():
        sum_ref[...] = jnp.zeros_like(sum_ref)

    sum_ref[...] += mm(returned_ref[...], tokens_ref[...])

    @pl.when(step == STEPS - 1)
    def _():
        kept = sum_ref[...].astype(BF16) * mask_ref[...]
        flat = mm(rep_ref[...], kept, 0, 0).astype(BF16)
        grad_ref[...] = mm(order_ref[...], flat, 1, 1).astype(BF16)


def first_grad(returned, tokens, mask, rep, order):
    return pl.pallas_call(
        first_grad_kernel,
        grid=(STEPS,),
        in_specs=[
            columns(FEAT),
            token_rows(),
            whole((FEAT, FEAT)),
            whole((FEAT, 128)),
            whole((FEAT, FEAT)),
        ],
        out_specs=whole((FEAT, 128)),
        out_shape=struct((FEAT, 128)),
        scratch_shapes=[pltpu.VMEM((FEAT, FEAT), F32)],
        compiler_params=PARAMS,
        cost_estimate=cost(2 * TOK * FEAT * FEAT, 3 << 20),
        name="first_grad",
    )(returned, tokens, mask, rep, order)


def token_grad_kernel(returned_ref, matrix_ref, out_ref):
    out_ref[...] = mm(returned_ref[...], matrix_ref[...], 0, 0).astype(BF16)


def token_gradient(returned, matrix):
    return pl.pallas_call(
        token_grad_kernel,
        grid=(STEPS,),
        in_specs=[columns(FEAT), whole((FEAT, FEAT))],
        out_specs=token_rows(),
        out_shape=struct((TOK, FEAT)),
        compiler_params=PARAMS,
        cost_estimate=cost(2 * TOK * FEAT * FEAT, 3 << 20),
        name="token_gradient",
    )(returned, matrix)


def gather_pieces(x):
    for bit in DP_ORDER:
        other = lax.ppermute(x, "dp", [(i, i ^ bit) for i in range(16)])
        x = jnp.concatenate([x, other], axis=0)
    return x


def offset(place):
    total = jnp.zeros_like(place)
    for level, bit in enumerate(DP_ORDER):
        total = total + ((place >> level) & 1) * bit
    return total


def to_tensor(x):
    return lax.all_to_all(x, "tensor", split_axis=0, concat_axis=0, tiled=True)


def grid_of(rows, cols):
    return (
        lax.broadcasted_iota(jnp.int32, (rows, cols), 0),
        lax.broadcasted_iota(jnp.int32, (rows, cols), 1),
    )


def local(
    patches, visible, block_perm, first_left, first_right, second_right, second_left, cotangent
):
    me = lax.axis_index("dp").astype(jnp.int32)

    left = gather_pieces(
        jnp.concatenate([first_left.reshape(24, BS), second_left.reshape(24, BS)], axis=0)
    )
    two = second_right.reshape(2, 3, 16, NB).transpose(1, 2, 0, 3).reshape(48, 128)
    one = first_right.reshape(24, HB)
    right = jnp.concatenate([two, one[:, :128], one[:, 128:]], axis=0)

    tokens = pick(patches, visible)

    row, col = grid_of(768, FEAT)
    piece, which, block, rest = row // 48, (row // 24) % 2, (row // 6) % 4, row % 6
    source_row = 6 * (me ^ offset(piece)) + rest
    place_one = ((which == 0) & (block == col // BS) & (source_row == col % BS)).astype(BF16)
    col, row = grid_of(FEAT, 768)
    piece, which, block, rest = row // 48, (row // 24) % 2, (row // 6) % 4, row % 6
    source_row = 6 * (me ^ offset(piece)) + rest
    place_two = ((which == 1) & (block == col % LB) & (source_row == col // LB)).astype(BF16)
    row, col = grid_of(FEAT, FEAT)
    mask = (row % LB == col // BS).astype(BF16)
    order = ((row % LB == col // BS) & (row // LB == col % BS)).astype(BF16)
    owner = (((row // 4) % POS == col // NB) & ((row // 24) * 4 + row % 4 == col % NB)).astype(BF16)
    wanted = jnp.tile(block_perm, POS)[:, None]
    perm = ((row // NB == (col // 4) % POS) & ((col // 24) * 4 + col % 4 == wanted)).astype(BF16)
    row, col = grid_of(FEAT, 128)
    rep = (row // LB == col).astype(BF16)
    fold = (row % BS == col).astype(BF16)
    row, col = grid_of(BS, FEAT)
    spread = (row == col % BS).astype(BF16)

    matrix_one, section_one = block_map(
        up_kernel, "first_map", tokens, left, place_one, rep[:, :BS], mask
    )
    arrived = to_tensor(section_one)
    matrix_two, back_grad = block_map(
        down_kernel, "second_map_back", cotangent, left, place_two, spread, mask
    )
    arrived_grad = to_tensor(back_grad)

    right = gather_pieces(right).reshape(16, 96, 128)
    right = jnp.take(right, offset(jnp.arange(16, dtype=jnp.int32) ^ me), axis=0)
    right_two = (
        right[:, :48].reshape(16, 3, 16, 2, NB).transpose(3, 1, 0, 2, 4).reshape(POS, HB, NB)
    )
    right_one = (
        right[:, 48:].reshape(16, 2, POS, 4, 128).transpose(2, 0, 3, 1, 4).reshape(POS, NB, HB)
    )

    mixed, act, slope, leaving = mix_forward(arrived, perm, right_one, right_two)
    returned = to_tensor(leaving)
    leaving_grad, grad_right_one, grad_right_two = mix_backward(
        arrived_grad, perm, right_one, right_two, mixed, act, slope, owner
    )
    returned_grad = to_tensor(leaving_grad)
    output, grad_left_two = output_and_grad(returned, matrix_two, cotangent, mask, fold)
    grad_left_one = first_grad(returned_grad, tokens, mask, rep, order)
    token_grad = token_gradient(returned_grad, matrix_one)

    shares = jnp.concatenate(
        [
            grad_left_one.reshape(16, 24, 128),
            grad_left_two.reshape(16, 24, 128),
            grad_right_one[:, :128].reshape(16, 24, 128),
            grad_right_one[:, 128:].reshape(16, 24, 128),
            grad_right_two.reshape(16, 48, 128),
        ],
        axis=1,
    )
    shares = lax.all_to_all(shares, "dp", split_axis=0, concat_axis=0, tiled=True)
    total = jnp.sum(shares.astype(F32), axis=0)
    left_total = total[:48, :BS].reshape(2, 6, LB, BS).transpose(0, 2, 1, 3)
    one_total = total[48:96].reshape(2, POS, 4, 128).transpose(1, 2, 0, 3).reshape(POS, 4, HB)
    two_total = total[96:].reshape(3, 16, 2, NB).transpose(2, 0, 1, 3).reshape(POS, 16, NB)
    return (output, token_grad, left_total[0], one_total, two_total, left_total[1])


def solution(mesh):
    placed = (
        P("dp", None, "tensor"),
        P("dp", None),
        P(),
        P("tensor", "dp", None),
        P("tensor", "dp", None),
        P("tensor", "dp", None),
        P("tensor", "dp", None),
        P("dp", "tensor"),
    )
    return jax.shard_map(
        local,
        mesh=mesh,
        in_specs=placed,
        out_specs=(
            P("dp", "tensor"),
            P("dp", "tensor"),
            P("tensor", "dp", None),
            P("tensor", "dp", None),
            P("tensor", "dp", None),
            P("tensor", "dp", None),
        ),
        check_vma=False,
    )
```

```python
import math

import jax
import jax.numpy as jnp
from jax import lax
from jax.experimental import pallas as pl
from jax.experimental.pallas import tpu as pltpu
from jax.sharding import PartitionSpec as P

BF16 = jnp.bfloat16
F32 = jnp.float32
NB, BS, HB = 64, 96, 256
POS = 6
LB = 4
FEAT = LB * BS
TOK = 2048
PIECES = 16
ALL_ROWS = 768
TILE = 512
STEPS = TOK // TILE
WIDE = 1024
WIDE_STEPS = TOK // WIDE
ROOT_RATIO = math.sqrt(2.0 / math.pi)
DP_ORDER = (1, 8, 4, 2)
PARAMS = pltpu.CompilerParams(vmem_limit_bytes=63 * 1024 * 1024)


def mm(lhs, rhs, left_dim=1, right_dim=0):
    return lax.dot_general(
        lhs, rhs, (((left_dim,), (right_dim,)), ((), ())), preferred_element_type=F32
    )


def whole(shape):
    return pl.BlockSpec(shape, lambda *_: (0,) * len(shape))


def columns(rows, tile=TILE):
    return pl.BlockSpec((rows, tile), lambda step: (0, step))


def token_rows():
    return pl.BlockSpec((WIDE, FEAT), lambda step: (step, 0))


def piece_rows(part):
    return pl.BlockSpec((PIECES, 48, 128), lambda *_: (0, part, 0))


def struct(shape, dtype=BF16):
    return jax.ShapeDtypeStruct(shape, dtype)


def cost(flops, moved):
    return pl.CostEstimate(flops=flops, bytes_accessed=moved, transcendentals=0)


def offset(place):
    return sum(((place >> level) & 1) * bit for level, bit in enumerate(DP_ORDER))


def prepare_kernel(
    perm_ref,
    visible_ref,
    patches_ref,
    tokens_ref,
    place_one_ref,
    place_two_ref,
    owner_ref,
    mix_ref,
    mask_ref,
    rep_ref,
    fold_ref,
    spread_ref,
):
    images, patch_count, _ = patches_ref.shape
    vis = visible_ref.shape[2]
    for image in range(images):
        wanted = visible_ref[image]
        chosen = lax.broadcasted_iota(jnp.int32, (patch_count, vis), 0) == wanted
        rows = mm(chosen.astype(F32).astype(BF16), patches_ref[image], 0, 0)
        tokens_ref[image * vis : (image + 1) * vis, :] = rows.astype(BF16)

    @pl.when(pl.program_id(0) == 0)
    def _():
        def tall(rows):
            return lax.broadcasted_iota(jnp.int32, (rows, 1), 0)

        def wide(cols):
            return lax.broadcasted_iota(jnp.int32, (1, cols), 1)

        def equal(left, right):
            return (left == right).astype(F32).astype(BF16)

        def parts(row, inner):
            outer = lax.div(row, inner)
            return outer, row - outer * inner

        def left_keys(row):
            piece, rest = parts(row, 48)
            which, rest = parts(rest, 24)
            near, block = parts(rest, LB)
            return which, piece * 6 + near, block

        which, source, block = left_keys(tall(ALL_ROWS))
        place_one_ref[...] = equal(jnp.where(which == 0, block * BS + source, -1), wide(FEAT))
        place_two_ref[...] = equal(jnp.where(which == 1, source * LB + block, -1), wide(FEAT))

        piece, rest = parts(tall(ALL_ROWS), 48)
        half, rest = parts(rest, 24)
        pos, near = parts(rest, 4)
        key = half * FEAT + pos * NB + piece * 4 + near
        owner_ref[...] = equal(key, wide(ALL_ROWS))

        piece, rest = parts(tall(FEAT), 24)
        pos, near = parts(rest, 4)
        blocks = jnp.concatenate([perm_ref[...]] * POS, axis=1)
        at, _ = parts(wide(FEAT), NB)
        mix_ref[...] = equal(pos * NB + piece * 4 + near, at * NB + blocks)

        outer, inner = parts(tall(FEAT), LB)
        block, within = parts(wide(FEAT), BS)
        mask_ref[...] = equal(inner, block)
        rep_ref[...] = equal(outer, wide(128))
        _, row_within = parts(tall(FEAT), BS)
        fold_ref[...] = equal(row_within, wide(128))
        spread_ref[...] = equal(tall(128), within)


def prepare(block_perm, visible, patches):
    images, patch_count, feats = patches.shape
    vis = visible.shape[1]
    group = 8
    shapes = [
        (ALL_ROWS, FEAT),
        (ALL_ROWS, FEAT),
        (ALL_ROWS, ALL_ROWS),
        (FEAT, FEAT),
        (FEAT, FEAT),
        (FEAT, 128),
        (FEAT, 128),
        (128, FEAT),
    ]
    return pl.pallas_call(
        prepare_kernel,
        grid=(images // group,),
        in_specs=[
            whole((1, NB)),
            pl.BlockSpec((group, 1, vis), lambda step: (step, 0, 0)),
            pl.BlockSpec((group, patch_count, feats), lambda step: (step, 0, 0)),
        ],
        out_specs=[pl.BlockSpec((group * vis, feats), lambda step: (step, 0))]
        + [whole(shape) for shape in shapes],
        out_shape=[struct((images * vis, feats))] + [struct(shape) for shape in shapes],
        compiler_params=PARAMS,
        cost_estimate=cost(2 * TOK * patch_count * feats, 12 << 20),
        name="prepare",
    )(block_perm[None, :], visible[:, None, :], patches)


def up_kernel(tokens_ref, pieces_ref, place_ref, rep_ref, mask_ref, matrix_ref, section_ref):
    @pl.when(pl.program_id(0) == 0)
    def _():
        pieces = pieces_ref[...].reshape(ALL_ROWS, 128)
        flat = mm(pieces, place_ref[...], 0, 0).astype(BF16)
        matrix_ref[...] = mm(rep_ref[...], flat).astype(BF16) * mask_ref[...]

    section_ref[...] = mm(matrix_ref[...], tokens_ref[...], 1, 1).astype(BF16)


def down_kernel(upstream_ref, pieces_ref, place_ref, spread_ref, mask_ref, matrix_ref, section_ref):
    @pl.when(pl.program_id(0) == 0)
    def _():
        pieces = pieces_ref[...].reshape(ALL_ROWS, 128)
        tall = mm(place_ref[...], pieces, 0, 0).astype(BF16)
        matrix_ref[...] = mm(tall, spread_ref[...]).astype(BF16) * mask_ref[...]

    section_ref[...] = mm(matrix_ref[...], upstream_ref[...], 1, 1).astype(BF16)


def block_map(kernel, name, rows, pieces, place, spread, mask):
    return pl.pallas_call(
        kernel,
        grid=(WIDE_STEPS,),
        in_specs=[
            token_rows(),
            piece_rows(0),
            whole(place.shape),
            whole(spread.shape),
            whole(mask.shape),
        ],
        out_specs=[whole((FEAT, FEAT)), columns(FEAT, WIDE)],
        out_shape=[struct((FEAT, FEAT)), struct((FEAT, TOK))],
        compiler_params=PARAMS,
        cost_estimate=cost(2 * TOK * FEAT * FEAT * 3, 5 << 20),
        name=name,
    )(rows, pieces, place, spread, mask)


def arrange_kernel(two_ref, one_ref, owner_ref, right_one_ref, right_two_ref):
    for pos in range(POS // 2):
        rows = two_ref[:, pos * 16 : pos * 16 + 16, :].reshape(HB, 128)
        right_two_ref[pos] = rows[:, :NB]
        right_two_ref[pos + POS // 2] = rows[:, NB:]
    both = mm(owner_ref[...], one_ref[...].reshape(ALL_ROWS, 128), 0, 0).astype(BF16)
    for pos in range(POS):
        right_one_ref[pos] = jnp.concatenate(
            [both[pos * NB : pos * NB + NB], both[FEAT + pos * NB : FEAT + pos * NB + NB]], axis=1
        )


def arrange(pieces, owner):
    return pl.pallas_call(
        arrange_kernel,
        grid=(1,),
        in_specs=[piece_rows(1), piece_rows(2), whole((ALL_ROWS, ALL_ROWS))],
        out_specs=[whole((POS, NB, HB)), whole((POS, HB, NB))],
        out_shape=[struct((POS, NB, HB)), struct((POS, HB, NB))],
        compiler_params=PARAMS,
        cost_estimate=cost(2 * ALL_ROWS * ALL_ROWS * 128, 3 << 20),
        name="arrange",
    )(pieces, pieces, owner)


def forward_kernel(
    arrived_ref, perm_ref, right_one_ref, right_two_ref, mixed_ref, act_ref, slope_ref, leaving_ref, own_ref
):
    mixed_ref[...] = mm(perm_ref[...], arrived_ref[...], 0, 0).astype(BF16)
    for pos in range(POS):
        rows = slice(pos * NB, (pos + 1) * NB)
        hidden_rows = slice(pos * HB, (pos + 1) * HB)
        hidden = mm(right_one_ref[pos], mixed_ref[rows, :], 0, 0)
        square = hidden * hidden
        tangent = jnp.tanh(hidden * (ROOT_RATIO + (ROOT_RATIO * 0.044715) * square))
        half = 0.5 * hidden
        act = (half + half * tangent).astype(BF16)
        slope = (0.5 + 0.5 * tangent) + half * (1.0 - tangent * tangent) * (
            ROOT_RATIO + (ROOT_RATIO * 3.0 * 0.044715) * square
        )
        act_ref[hidden_rows, :] = act
        slope_ref[hidden_rows, :] = slope.astype(BF16)
        own_ref[rows, :] = mm(right_two_ref[pos], act, 0, 0).astype(BF16)
    leaving_ref[...] = mm(perm_ref[...], own_ref[...]).astype(BF16)


def mix_forward(arrived, perm, right_one, right_two):
    return pl.pallas_call(
        forward_kernel,
        grid=(STEPS,),
        in_specs=[
            columns(FEAT),
            whole((FEAT, FEAT)),
            whole((POS, NB, HB)),
            whole((POS, HB, NB)),
        ],
        out_specs=[columns(FEAT), columns(POS * HB), columns(POS * HB), columns(FEAT)],
        out_shape=[
            struct((FEAT, TOK)),
            struct((POS * HB, TOK)),
            struct((POS * HB, TOK)),
            struct((FEAT, TOK)),
        ],
        scratch_shapes=[pltpu.VMEM((FEAT, TILE), BF16)],
        compiler_params=PARAMS,
        cost_estimate=cost(12 * TOK * FEAT * FEAT, 17 << 20),
        name="mix_forward",
    )(arrived, perm, right_one, right_two)


def backward_kernel(
    me_ref,
    arrived_ref,
    perm_ref,
    right_one_ref,
    right_two_ref,
    mixed_ref,
    act_ref,
    slope_ref,
    owner_ref,
    leaving_ref,
    shares_ref,
    grads_ref,
    own_ref,
    sum_one_ref,
    sum_two_ref,
    pair_ref,
    one_ref,
):
    step = pl.program_id(0)

    @pl.when(step == 0)
    def _():
        sum_one_ref[...] = jnp.zeros_like(sum_one_ref)
        sum_two_ref[...] = jnp.zeros_like(sum_two_ref)

    grads_ref[...] = mm(perm_ref[...], arrived_ref[...], 0, 0).astype(BF16)
    for pos in range(POS):
        rows = slice(pos * NB, (pos + 1) * NB)
        hidden_rows = slice(pos * HB, (pos + 1) * HB)
        grad_act = mm(right_two_ref[pos], grads_ref[rows, :])
        grad_hidden = (grad_act * slope_ref[hidden_rows, :].astype(F32)).astype(BF16)
        own_ref[rows, :] = mm(right_one_ref[pos], grad_hidden).astype(BF16)
        sum_one_ref[rows, :] += mm(mixed_ref[rows, :], grad_hidden, 1, 1)
        sum_two_ref[pos] += mm(act_ref[hidden_rows, :], grads_ref[rows, :], 1, 1)
    leaving_ref[...] = mm(perm_ref[...], own_ref[...]).astype(BF16)

    @pl.when(step == STEPS - 1)
    def _():
        me = me_ref[0]
        halves = jnp.concatenate([sum_one_ref[:, :128], sum_one_ref[:, 128:]], axis=0)
        one_ref[...] = mm(owner_ref[...], halves.astype(BF16)).astype(BF16)
        for pos in range(POS // 2):
            pair_ref[pos] = jnp.concatenate(
                [sum_two_ref[pos], sum_two_ref[pos + POS // 2]], axis=1
            )
        for piece in range(PIECES):
            of = me ^ offset(piece)
            start = pl.multiple_of(of * 16, 16)
            for pos in range(POS // 2):
                shares_ref[piece * 96 + pos * 16 : piece * 96 + pos * 16 + 16, :] = pair_ref[
                    pos, pl.ds(start, 16), :
                ].astype(BF16)
            start = pl.multiple_of(of * 48, 16)
            shares_ref[piece * 96 + 48 : piece * 96 + 96, :] = one_ref[pl.ds(start, 48), :]


def mix_backward(me, arrived, perm, right_one, right_two, mixed, act, slope, owner):
    return pl.pallas_call(
        backward_kernel,
        grid=(STEPS,),
        in_specs=[
            pl.BlockSpec(memory_space=pltpu.SMEM),
            columns(FEAT),
            whole((FEAT, FEAT)),
            whole((POS, NB, HB)),
            whole((POS, HB, NB)),
            columns(FEAT),
            columns(POS * HB),
            columns(POS * HB),
            whole((ALL_ROWS, ALL_ROWS)),
        ],
        out_specs=[columns(FEAT), whole((PIECES * 96, 128))],
        out_shape=[struct((FEAT, TOK)), struct((PIECES * 96, 128))],
        scratch_shapes=[
            pltpu.VMEM((FEAT, TILE), BF16),
            pltpu.VMEM((FEAT, TILE), BF16),
            pltpu.VMEM((FEAT, HB), F32),
            pltpu.VMEM((POS, HB, NB), F32),
            pltpu.VMEM((POS // 2, HB, 2 * NB), F32),
            pltpu.VMEM((ALL_ROWS, 128), BF16),
        ],
        compiler_params=PARAMS,
        cost_estimate=cost(20 * TOK * FEAT * FEAT, 17 << 20),
        name="mix_backward",
    )(me, arrived, perm, right_one, right_two, mixed, act, slope, owner)


def output_kernel(returned_ref, matrix_ref, upstream_ref, mask_ref, fold_ref, out_ref, grad_ref, sum_ref):
    step = pl.program_id(0)

    @pl.when(step == 0)
    def _():
        sum_ref[...] = jnp.zeros_like(sum_ref)

    out_ref[...] = mm(returned_ref[...], matrix_ref[...], 0, 0).astype(BF16)
    sum_ref[...] += mm(returned_ref[...], upstream_ref[...])

    @pl.when(step == WIDE_STEPS - 1)
    def _():
        kept = sum_ref[...].astype(BF16) * mask_ref[...]
        grad_ref[...] = mm(kept, fold_ref[...]).astype(BF16)


def output_and_grad(returned, matrix, upstream, mask, fold):
    return pl.pallas_call(
        output_kernel,
        grid=(WIDE_STEPS,),
        in_specs=[
            columns(FEAT, WIDE),
            whole((FEAT, FEAT)),
            token_rows(),
            whole((FEAT, FEAT)),
            whole((FEAT, 128)),
        ],
        out_specs=[token_rows(), whole((FEAT, 128))],
        out_shape=[struct((TOK, FEAT)), struct((FEAT, 128))],
        scratch_shapes=[pltpu.VMEM((FEAT, FEAT), F32)],
        compiler_params=PARAMS,
        cost_estimate=cost(4 * TOK * FEAT * FEAT, 5 << 20),
        name="output_and_grad",
    )(returned, matrix, upstream, mask, fold)


def first_grad_kernel(
    returned_ref,
    tokens_ref,
    mask_ref,
    rep_ref,
    order_one_ref,
    order_two_ref,
    second_ref,
    shares_ref,
    sum_ref,
):
    step = pl.program_id(0)

    @pl.when(step == 0)
    def _():
        sum_ref[...] = jnp.zeros_like(sum_ref)

    sum_ref[...] += mm(returned_ref[...], tokens_ref[...])

    @pl.when(step == WIDE_STEPS - 1)
    def _():
        kept = sum_ref[...].astype(BF16) * mask_ref[...]
        flat = mm(rep_ref[...], kept, 0, 0).astype(BF16)
        shares = mm(order_one_ref[...], flat, 1, 1) + mm(order_two_ref[...], second_ref[...])
        shares_ref[...] = shares.astype(BF16)


def first_grad(returned, tokens, mask, rep, order_one, order_two, second):
    return pl.pallas_call(
        first_grad_kernel,
        grid=(WIDE_STEPS,),
        in_specs=[
            columns(FEAT, WIDE),
            token_rows(),
            whole((FEAT, FEAT)),
            whole((FEAT, 128)),
            whole((ALL_ROWS, FEAT)),
            whole((ALL_ROWS, FEAT)),
            whole((FEAT, 128)),
        ],
        out_specs=whole((ALL_ROWS, 128)),
        out_shape=struct((ALL_ROWS, 128)),
        scratch_shapes=[pltpu.VMEM((FEAT, FEAT), F32)],
        compiler_params=PARAMS,
        cost_estimate=cost(2 * TOK * FEAT * FEAT, 3 << 20),
        name="first_grad",
    )(returned, tokens, mask, rep, order_one, order_two, second)


def token_grad_kernel(returned_ref, matrix_ref, out_ref):
    out_ref[...] = mm(returned_ref[...], matrix_ref[...], 0, 0).astype(BF16)


def token_gradient(returned, matrix):
    return pl.pallas_call(
        token_grad_kernel,
        grid=(WIDE_STEPS,),
        in_specs=[columns(FEAT, WIDE), whole((FEAT, FEAT))],
        out_specs=token_rows(),
        out_shape=struct((TOK, FEAT)),
        compiler_params=PARAMS,
        cost_estimate=cost(2 * TOK * FEAT * FEAT, 3 << 20),
        name="token_gradient",
    )(returned, matrix)


def exchange(x, bit):
    return lax.ppermute(x, "dp", [(i, i ^ bit) for i in range(PIECES)])


def halved(x, bit):
    rows = x.shape[0] // 2
    return (x[:rows].astype(F32) + exchange(x[rows:], bit).astype(F32)).astype(BF16)


def to_tensor(x):
    return lax.all_to_all(x, "tensor", split_axis=0, concat_axis=0, tiled=True)


def local(
    patches, visible, block_perm, first_left, first_right, second_right, second_left, cotangent
):
    tie = lax.optimization_barrier
    me = lax.axis_index("dp").astype(jnp.int32).reshape(1)

    left = jnp.concatenate([first_left.transpose(1, 0, 2), second_left.transpose(1, 0, 2)], axis=0)
    left = jnp.pad(left.reshape(48, BS), ((0, 0), (0, 128 - BS)))
    two = second_right.reshape(2, 3, 16, NB).transpose(1, 2, 0, 3).reshape(48, 128)
    one = first_right.reshape(24, HB)
    piece = jnp.concatenate([left, two, one[:, :128], one[:, 128:]], axis=0)
    pieces = jnp.broadcast_to(piece[None], (PIECES, 144, 128))
    pieces = lax.all_to_all(pieces, "dp", split_axis=0, concat_axis=0, tiled=True)

    tokens, place_one, place_two, owner, perm, mask, rep, fold, spread = prepare(
        block_perm, visible, patches
    )
    pieces, tokens = tie((pieces, tokens))

    matrix_one, section_one = block_map(
        up_kernel, "first_map", tokens, pieces, place_one, rep, mask
    )
    arrived = to_tensor(section_one)
    matrix_two, back_grad = block_map(
        down_kernel, "second_map_back", cotangent, pieces, place_two, spread, mask
    )
    right_one, right_two = arrange(pieces, owner)
    arrived, back_grad, right_one = tie((arrived, back_grad, right_one))
    arrived_grad = to_tensor(back_grad)

    mixed, act, slope, leaving = mix_forward(arrived, perm, right_one, right_two)
    leaving, arrived_grad = tie((leaving, arrived_grad))
    returned = to_tensor(leaving)
    leaving_grad, right_shares = mix_backward(
        me, arrived_grad, perm, right_one, right_two, mixed, act, slope, owner
    )
    right_shares = halved(right_shares, DP_ORDER[3])
    returned, leaving_grad, right_shares = tie((returned, leaving_grad, right_shares))
    returned_grad = to_tensor(leaving_grad)
    output, grad_left_two = output_and_grad(returned, matrix_two, cotangent, mask, fold)
    right_shares, grad_left_two = tie((right_shares, grad_left_two))
    right_shares = halved(right_shares, DP_ORDER[2])
    right_shares = halved(right_shares, DP_ORDER[1])

    left_held = first_grad(
        returned_grad, tokens, mask, rep, place_one, place_two, grad_left_two
    )
    left_shares = lax.all_to_all(left_held, "dp", split_axis=0, concat_axis=0, tiled=True)
    returned_grad, left_held = tie((returned_grad, left_held))
    token_grad = token_gradient(returned_grad, matrix_one)

    right_total = halved(right_shares, DP_ORDER[0]).astype(F32)

    left_total = jnp.sum(left_shares.reshape(PIECES, 48, 128).astype(F32), axis=0)[:, :BS]
    left_total = left_total.reshape(2, 6, LB, BS).transpose(0, 2, 1, 3)
    two_total = right_total[:48].reshape(3, 16, 2, NB).transpose(2, 0, 1, 3).reshape(POS, 16, NB)
    one_total = jnp.concatenate([right_total[48:72], right_total[72:]], axis=1)
    one_total = one_total.reshape(POS, 4, HB)
    return (output, token_grad, left_total[0], one_total, two_total, left_total[1])


def solution(mesh):
    placed = (
        P("dp", None, "tensor"),
        P("dp", None),
        P(),
        P("tensor", "dp", None),
        P("tensor", "dp", None),
        P("tensor", "dp", None),
        P("tensor", "dp", None),
        P("dp", "tensor"),
    )
    return jax.shard_map(
        local,
        mesh=mesh,
        in_specs=placed,
        out_specs=(
            P("dp", "tensor"),
            P("dp", "tensor"),
            P("tensor", "dp", None),
            P("tensor", "dp", None),
            P("tensor", "dp", None),
            P("tensor", "dp", None),
        ),
        check_vma=False,
    )
```

```python
import math

import jax
import jax.numpy as jnp
from jax import lax
from jax.experimental import pallas as pl
from jax.experimental.pallas import tpu as pltpu
from jax.sharding import PartitionSpec as P

BF16 = jnp.bfloat16
F32 = jnp.float32
NB, BS, HB = 64, 96, 256
POS = 6
LB = 4
FEAT = LB * BS
TOK = 2048
PIECES = 16
ALL_ROWS = 768
TILE = 1024
STEPS = TOK // TILE
WIDE = 1024
WIDE_STEPS = TOK // WIDE
ROOT_RATIO = math.sqrt(2.0 / math.pi)
DP_ORDER = (1, 8, 4, 2)
PARAMS = pltpu.CompilerParams(vmem_limit_bytes=63 * 1024 * 1024 + 512 * 1024)


def mm(lhs, rhs, left_dim=1, right_dim=0):
    return lax.dot_general(
        lhs, rhs, (((left_dim,), (right_dim,)), ((), ())), preferred_element_type=F32
    )


def whole(shape):
    return pl.BlockSpec(shape, lambda *_: (0,) * len(shape))


def columns(rows, tile=TILE):
    return pl.BlockSpec((rows, tile), lambda step: (0, step))


def token_rows():
    return pl.BlockSpec((WIDE, FEAT), lambda step: (step, 0))


def piece_rows(part):
    return pl.BlockSpec((PIECES, 48, 128), lambda *_: (0, part, 0))


def struct(shape, dtype=BF16):
    return jax.ShapeDtypeStruct(shape, dtype)


def cost(flops, moved):
    return pl.CostEstimate(flops=flops, bytes_accessed=moved, transcendentals=0)


def offset(place):
    return sum(((place >> level) & 1) * bit for level, bit in enumerate(DP_ORDER))


def prepare_kernel(
    perm_ref,
    visible_ref,
    patches_ref,
    tokens_ref,
    place_one_ref,
    place_two_ref,
    owner_ref,
    mix_ref,
    mask_ref,
    rep_ref,
    fold_ref,
    spread_ref,
):
    images, patch_count, _ = patches_ref.shape
    vis = visible_ref.shape[2]
    for image in range(images):
        wanted = visible_ref[image]
        chosen = lax.broadcasted_iota(jnp.int32, (patch_count, vis), 0) == wanted
        rows = mm(chosen.astype(F32).astype(BF16), patches_ref[image], 0, 0)
        tokens_ref[image * vis : (image + 1) * vis, :] = rows.astype(BF16)

    @pl.when(pl.program_id(0) == 0)
    def _():
        def tall(rows):
            return lax.broadcasted_iota(jnp.int32, (rows, 1), 0)

        def wide(cols):
            return lax.broadcasted_iota(jnp.int32, (1, cols), 1)

        def equal(left, right):
            return (left == right).astype(F32).astype(BF16)

        def parts(row, inner):
            outer = lax.div(row, inner)
            return outer, row - outer * inner

        def left_keys(row):
            piece, rest = parts(row, 48)
            which, rest = parts(rest, 24)
            near, block = parts(rest, LB)
            return which, piece * 6 + near, block

        which, source, block = left_keys(tall(ALL_ROWS))
        place_one_ref[...] = equal(jnp.where(which == 0, block * BS + source, -1), wide(FEAT))
        place_two_ref[...] = equal(jnp.where(which == 1, source * LB + block, -1), wide(FEAT))

        piece, rest = parts(tall(ALL_ROWS), 48)
        half, rest = parts(rest, 24)
        pos, near = parts(rest, 4)
        key = half * FEAT + pos * NB + piece * 4 + near
        owner_ref[...] = equal(key, wide(ALL_ROWS))

        piece, rest = parts(tall(FEAT), 24)
        pos, near = parts(rest, 4)
        blocks = jnp.concatenate([perm_ref[...]] * POS, axis=1)
        at, _ = parts(wide(FEAT), NB)
        mix_ref[...] = equal(pos * NB + piece * 4 + near, at * NB + blocks)

        outer, inner = parts(tall(FEAT), LB)
        block, within = parts(wide(FEAT), BS)
        mask_ref[...] = equal(inner, block)
        rep_ref[...] = equal(outer, wide(128))
        _, row_within = parts(tall(FEAT), BS)
        fold_ref[...] = equal(row_within, wide(128))
        spread_ref[...] = equal(tall(128), within)


def prepare(block_perm, visible, patches):
    images, patch_count, feats = patches.shape
    vis = visible.shape[1]
    group = 8
    shapes = [
        (ALL_ROWS, FEAT),
        (ALL_ROWS, FEAT),
        (ALL_ROWS, ALL_ROWS),
        (FEAT, FEAT),
        (FEAT, FEAT),
        (FEAT, 128),
        (FEAT, 128),
        (128, FEAT),
    ]
    return pl.pallas_call(
        prepare_kernel,
        grid=(images // group,),
        in_specs=[
            whole((1, NB)),
            pl.BlockSpec((group, 1, vis), lambda step: (step, 0, 0)),
            pl.BlockSpec((group, patch_count, feats), lambda step: (step, 0, 0)),
        ],
        out_specs=[pl.BlockSpec((group * vis, feats), lambda step: (step, 0))]
        + [whole(shape) for shape in shapes],
        out_shape=[struct((images * vis, feats))] + [struct(shape) for shape in shapes],
        compiler_params=PARAMS,
        cost_estimate=cost(2 * TOK * patch_count * feats, 12 << 20),
        name="prepare",
    )(block_perm[None, :], visible[:, None, :], patches)


def up_kernel(tokens_ref, pieces_ref, place_ref, rep_ref, mask_ref, matrix_ref, section_ref):
    @pl.when(pl.program_id(0) == 0)
    def _():
        pieces = pieces_ref[...].reshape(ALL_ROWS, 128)
        flat = mm(pieces, place_ref[...], 0, 0).astype(BF16)
        matrix_ref[...] = mm(rep_ref[...], flat).astype(BF16) * mask_ref[...]

    section_ref[...] = mm(matrix_ref[...], tokens_ref[...], 1, 1).astype(BF16)


def down_kernel(upstream_ref, pieces_ref, place_ref, spread_ref, mask_ref, matrix_ref, section_ref):
    @pl.when(pl.program_id(0) == 0)
    def _():
        pieces = pieces_ref[...].reshape(ALL_ROWS, 128)
        tall = mm(place_ref[...], pieces, 0, 0).astype(BF16)
        matrix_ref[...] = mm(tall, spread_ref[...]).astype(BF16) * mask_ref[...]

    section_ref[...] = mm(matrix_ref[...], upstream_ref[...], 1, 1).astype(BF16)


def block_map(kernel, name, rows, pieces, place, spread, mask):
    return pl.pallas_call(
        kernel,
        grid=(WIDE_STEPS,),
        in_specs=[
            token_rows(),
            piece_rows(0),
            whole(place.shape),
            whole(spread.shape),
            whole(mask.shape),
        ],
        out_specs=[whole((FEAT, FEAT)), columns(FEAT, WIDE)],
        out_shape=[struct((FEAT, FEAT)), struct((FEAT, TOK))],
        compiler_params=PARAMS,
        cost_estimate=cost(2 * TOK * FEAT * FEAT * 3, 5 << 20),
        name=name,
    )(rows, pieces, place, spread, mask)


def arrange_kernel(two_ref, one_ref, owner_ref, right_one_ref, right_two_ref):
    for pos in range(POS // 2):
        rows = two_ref[:, pos * 16 : pos * 16 + 16, :].reshape(HB, 128)
        right_two_ref[pos] = rows[:, :NB]
        right_two_ref[pos + POS // 2] = rows[:, NB:]
    both = mm(owner_ref[...], one_ref[...].reshape(ALL_ROWS, 128), 0, 0).astype(BF16)
    for pos in range(POS):
        right_one_ref[pos] = jnp.concatenate(
            [both[pos * NB : pos * NB + NB], both[FEAT + pos * NB : FEAT + pos * NB + NB]], axis=1
        )


def arrange(pieces, owner):
    return pl.pallas_call(
        arrange_kernel,
        grid=(1,),
        in_specs=[piece_rows(1), piece_rows(2), whole((ALL_ROWS, ALL_ROWS))],
        out_specs=[whole((POS, NB, HB)), whole((POS, HB, NB))],
        out_shape=[struct((POS, NB, HB)), struct((POS, HB, NB))],
        compiler_params=PARAMS,
        cost_estimate=cost(2 * ALL_ROWS * ALL_ROWS * 128, 3 << 20),
        name="arrange",
    )(pieces, pieces, owner)


def forward_kernel(
    arrived_ref, perm_ref, right_one_ref, right_two_ref, mixed_ref, act_ref, slope_ref, leaving_ref, own_ref
):
    mixed_ref[...] = mm(perm_ref[...], arrived_ref[...], 0, 0).astype(BF16)
    for pos in range(POS):
        rows = slice(pos * NB, (pos + 1) * NB)
        hidden_rows = slice(pos * HB, (pos + 1) * HB)
        hidden = mm(right_one_ref[pos], mixed_ref[rows, :], 0, 0)
        square = hidden * hidden
        tangent = jnp.tanh(hidden * (ROOT_RATIO + (ROOT_RATIO * 0.044715) * square))
        half = 0.5 * hidden
        act = (half + half * tangent).astype(BF16)
        slope = (0.5 + 0.5 * tangent) + half * (1.0 - tangent * tangent) * (
            ROOT_RATIO + (ROOT_RATIO * 3.0 * 0.044715) * square
        )
        act_ref[hidden_rows, :] = act
        slope_ref[hidden_rows, :] = slope.astype(BF16)
        own_ref[rows, :] = mm(right_two_ref[pos], act, 0, 0).astype(BF16)
    leaving_ref[...] = mm(perm_ref[...], own_ref[...]).astype(BF16)


def mix_forward(arrived, perm, right_one, right_two):
    return pl.pallas_call(
        forward_kernel,
        grid=(STEPS,),
        in_specs=[
            columns(FEAT),
            whole((FEAT, FEAT)),
            whole((POS, NB, HB)),
            whole((POS, HB, NB)),
        ],
        out_specs=[columns(FEAT), columns(POS * HB), columns(POS * HB), columns(FEAT)],
        out_shape=[
            struct((FEAT, TOK)),
            struct((POS * HB, TOK)),
            struct((POS * HB, TOK)),
            struct((FEAT, TOK)),
        ],
        scratch_shapes=[pltpu.VMEM((FEAT, TILE), BF16)],
        compiler_params=PARAMS,
        cost_estimate=cost(12 * TOK * FEAT * FEAT, 17 << 20),
        name="mix_forward",
    )(arrived, perm, right_one, right_two)


def backward_kernel(
    me_ref,
    arrived_ref,
    perm_ref,
    right_one_ref,
    right_two_ref,
    mixed_ref,
    act_ref,
    slope_ref,
    owner_ref,
    leaving_ref,
    kept_ref,
    sent_ref,
    grads_ref,
    own_ref,
    sum_one_ref,
    sum_two_ref,
    pair_ref,
    one_ref,
):
    step = pl.program_id(0)

    @pl.when(step == 0)
    def _():
        sum_one_ref[...] = jnp.zeros_like(sum_one_ref)
        sum_two_ref[...] = jnp.zeros_like(sum_two_ref)

    grads_ref[...] = mm(perm_ref[...], arrived_ref[...], 0, 0).astype(BF16)
    for pos in range(POS):
        rows = slice(pos * NB, (pos + 1) * NB)
        hidden_rows = slice(pos * HB, (pos + 1) * HB)
        grad_act = mm(right_two_ref[pos], grads_ref[rows, :])
        grad_hidden = (grad_act * slope_ref[hidden_rows, :].astype(F32)).astype(BF16)
        own_ref[rows, :] = mm(right_one_ref[pos], grad_hidden).astype(BF16)
        sum_one_ref[rows, :] += mm(mixed_ref[rows, :], grad_hidden, 1, 1)
        sum_two_ref[pos] += mm(act_ref[hidden_rows, :], grads_ref[rows, :], 1, 1)
    leaving_ref[...] = mm(perm_ref[...], own_ref[...]).astype(BF16)

    @pl.when(step == STEPS - 1)
    def _():
        me = me_ref[0]
        halves = jnp.concatenate([sum_one_ref[:, :128], sum_one_ref[:, 128:]], axis=0)
        one_ref[...] = mm(owner_ref[...], halves.astype(BF16)).astype(BF16)
        for pos in range(POS // 2):
            pair_ref[pos] = jnp.concatenate(
                [sum_two_ref[pos], sum_two_ref[pos + POS // 2]], axis=1
            )
        for piece in range(PIECES):
            of = me ^ offset(piece)
            start = pl.multiple_of(of * 16, 16)
            shares_ref = (kept_ref, sent_ref)[piece // 8]
            at = piece % 8 * 96
            for pos in range(POS // 2):
                shares_ref[at + pos * 16 : at + pos * 16 + 16, :] = pair_ref[
                    pos, pl.ds(start, 16), :
                ].astype(BF16)
            start = pl.multiple_of(of * 48, 16)
            shares_ref[at + 48 : at + 96, :] = one_ref[pl.ds(start, 48), :]


def mix_backward(me, arrived, perm, right_one, right_two, mixed, act, slope, owner):
    return pl.pallas_call(
        backward_kernel,
        grid=(STEPS,),
        in_specs=[
            pl.BlockSpec(memory_space=pltpu.SMEM),
            columns(FEAT),
            whole((FEAT, FEAT)),
            whole((POS, NB, HB)),
            whole((POS, HB, NB)),
            columns(FEAT),
            columns(POS * HB),
            columns(POS * HB),
            whole((ALL_ROWS, ALL_ROWS)),
        ],
        out_specs=[columns(FEAT), whole((ALL_ROWS, 128)), whole((ALL_ROWS, 128))],
        out_shape=[struct((FEAT, TOK)), struct((ALL_ROWS, 128)), struct((ALL_ROWS, 128))],
        scratch_shapes=[
            pltpu.VMEM((FEAT, TILE), BF16),
            pltpu.VMEM((FEAT, TILE), BF16),
            pltpu.VMEM((FEAT, HB), F32),
            pltpu.VMEM((POS, HB, NB), F32),
            pltpu.VMEM((POS // 2, HB, 2 * NB), F32),
            pltpu.VMEM((ALL_ROWS, 128), BF16),
        ],
        compiler_params=PARAMS,
        cost_estimate=cost(20 * TOK * FEAT * FEAT, 17 << 20),
        name="mix_backward",
    )(me, arrived, perm, right_one, right_two, mixed, act, slope, owner)


def second_grad_kernel(returned_ref, upstream_ref, mask_ref, fold_ref, grad_ref, sum_ref):
    step = pl.program_id(0)

    @pl.when(step == 0)
    def _():
        sum_ref[...] = jnp.zeros_like(sum_ref)

    sum_ref[...] += mm(returned_ref[...], upstream_ref[...])

    @pl.when(step == WIDE_STEPS - 1)
    def _():
        kept = sum_ref[...].astype(BF16) * mask_ref[...]
        grad_ref[...] = mm(kept, fold_ref[...]).astype(BF16)


def second_grad(returned, upstream, mask, fold):
    return pl.pallas_call(
        second_grad_kernel,
        grid=(WIDE_STEPS,),
        in_specs=[columns(FEAT, WIDE), token_rows(), whole((FEAT, FEAT)), whole((FEAT, 128))],
        out_specs=whole((FEAT, 128)),
        out_shape=struct((FEAT, 128)),
        scratch_shapes=[pltpu.VMEM((FEAT, FEAT), F32)],
        compiler_params=PARAMS,
        cost_estimate=cost(2 * TOK * FEAT * FEAT, 4 << 20),
        name="second_grad",
    )(returned, upstream, mask, fold)


def first_grad_kernel(
    returned_ref,
    tokens_ref,
    mask_ref,
    rep_ref,
    order_one_ref,
    order_two_ref,
    second_ref,
    shares_ref,
    sum_ref,
):
    step = pl.program_id(0)

    @pl.when(step == 0)
    def _():
        sum_ref[...] = jnp.zeros_like(sum_ref)

    sum_ref[...] += mm(returned_ref[...], tokens_ref[...])

    @pl.when(step == WIDE_STEPS - 1)
    def _():
        kept = sum_ref[...].astype(BF16) * mask_ref[...]
        flat = mm(rep_ref[...], kept, 0, 0).astype(BF16)
        shares = mm(order_one_ref[...], flat, 1, 1) + mm(order_two_ref[...], second_ref[...])
        shares_ref[...] = shares.astype(BF16)


def first_grad(returned, tokens, mask, rep, order_one, order_two, second):
    return pl.pallas_call(
        first_grad_kernel,
        grid=(WIDE_STEPS,),
        in_specs=[
            columns(FEAT, WIDE),
            token_rows(),
            whole((FEAT, FEAT)),
            whole((FEAT, 128)),
            whole((ALL_ROWS, FEAT)),
            whole((ALL_ROWS, FEAT)),
            whole((FEAT, 128)),
        ],
        out_specs=whole((ALL_ROWS, 128)),
        out_shape=struct((ALL_ROWS, 128)),
        scratch_shapes=[pltpu.VMEM((FEAT, FEAT), F32)],
        compiler_params=PARAMS,
        cost_estimate=cost(2 * TOK * FEAT * FEAT, 3 << 20),
        name="first_grad",
    )(returned, tokens, mask, rep, order_one, order_two, second)


def outputs_kernel(returned_ref, matrix_two_ref, returned_grad_ref, matrix_one_ref, out_ref, grad_ref):
    out_ref[...] = mm(returned_ref[...], matrix_two_ref[...], 0, 0).astype(BF16)
    grad_ref[...] = mm(returned_grad_ref[...], matrix_one_ref[...], 0, 0).astype(BF16)


def outputs(returned, matrix_two, returned_grad, matrix_one):
    return pl.pallas_call(
        outputs_kernel,
        grid=(WIDE_STEPS,),
        in_specs=[
            columns(FEAT, WIDE),
            whole((FEAT, FEAT)),
            columns(FEAT, WIDE),
            whole((FEAT, FEAT)),
        ],
        out_specs=[token_rows(), token_rows()],
        out_shape=[struct((TOK, FEAT)), struct((TOK, FEAT))],
        compiler_params=PARAMS,
        cost_estimate=cost(4 * TOK * FEAT * FEAT, 7 << 20),
        name="outputs",
    )(returned, matrix_two, returned_grad, matrix_one)


def exchange(x, bit):
    return lax.ppermute(x, "dp", [(i, i ^ bit) for i in range(PIECES)])


def added(one, other):
    return (one.astype(F32) + other.astype(F32)).astype(BF16)


def halved(x, bit):
    rows = x.shape[0] // 2
    return added(x[:rows], exchange(x[rows:], bit))


def to_tensor(x):
    return lax.all_to_all(x, "tensor", split_axis=0, concat_axis=0, tiled=True)


def local(
    patches, visible, block_perm, first_left, first_right, second_right, second_left, cotangent
):
    tie = lax.optimization_barrier
    me = lax.axis_index("dp").astype(jnp.int32).reshape(1)

    left = jnp.concatenate([first_left.transpose(1, 0, 2), second_left.transpose(1, 0, 2)], axis=0)
    left = jnp.pad(left.reshape(48, BS), ((0, 0), (0, 128 - BS)))
    two = second_right.reshape(2, 3, 16, NB).transpose(1, 2, 0, 3).reshape(48, 128)
    one = first_right.reshape(24, HB)
    piece = jnp.concatenate([left, two, one[:, :128], one[:, 128:]], axis=0)
    pieces = jnp.broadcast_to(piece[None], (PIECES, 144, 128))
    pieces = lax.all_to_all(pieces, "dp", split_axis=0, concat_axis=0, tiled=True)

    tokens, place_one, place_two, owner, perm, mask, rep, fold, spread = prepare(
        block_perm, visible, patches
    )
    pieces, tokens = tie((pieces, tokens))

    matrix_one, section_one = block_map(
        up_kernel, "first_map", tokens, pieces, place_one, rep, mask
    )
    arrived = to_tensor(section_one)
    matrix_two, back_grad = block_map(
        down_kernel, "second_map_back", cotangent, pieces, place_two, spread, mask
    )
    right_one, right_two = arrange(pieces, owner)
    arrived, back_grad, right_one = tie((arrived, back_grad, right_one))
    arrived_grad = to_tensor(back_grad)

    mixed, act, slope, leaving = mix_forward(arrived, perm, right_one, right_two)
    leaving, arrived_grad = tie((leaving, arrived_grad))
    returned = to_tensor(leaving)
    leaving_grad, kept, sent = mix_backward(
        me, arrived_grad, perm, right_one, right_two, mixed, act, slope, owner
    )
    right_shares = added(kept, exchange(sent, DP_ORDER[3]))
    returned, leaving_grad, right_shares = tie((returned, leaving_grad, right_shares))
    returned_grad = to_tensor(leaving_grad)
    grad_left_two = second_grad(returned, cotangent, mask, fold)
    right_shares, grad_left_two = tie((right_shares, grad_left_two))
    right_shares = halved(right_shares, DP_ORDER[2])
    right_shares = halved(right_shares, DP_ORDER[1])

    left_held = first_grad(
        returned_grad, tokens, mask, rep, place_one, place_two, grad_left_two
    )
    left_shares = lax.all_to_all(left_held, "dp", split_axis=0, concat_axis=0, tiled=True)
    returned_grad, right_shares, left_held = tie((returned_grad, right_shares, left_held))
    output, token_grad = outputs(returned, matrix_two, returned_grad, matrix_one)

    right_total = halved(right_shares, DP_ORDER[0]).astype(F32)

    left_total = jnp.sum(left_shares.reshape(PIECES, 48, 128).astype(F32), axis=0)[:, :BS]
    left_total = left_total.reshape(2, 6, LB, BS).transpose(0, 2, 1, 3)
    two_total = right_total[:48].reshape(3, 16, 2, NB).transpose(2, 0, 1, 3).reshape(POS, 16, NB)
    one_total = jnp.concatenate([right_total[48:72], right_total[72:]], axis=1)
    one_total = one_total.reshape(POS, 4, HB)
    return (output, token_grad, left_total[0], one_total, two_total, left_total[1])


def solution(mesh):
    placed = (
        P("dp", None, "tensor"),
        P("dp", None),
        P(),
        P("tensor", "dp", None),
        P("tensor", "dp", None),
        P("tensor", "dp", None),
        P("tensor", "dp", None),
        P("dp", "tensor"),
    )
    return jax.shard_map(
        local,
        mesh=mesh,
        in_specs=placed,
        out_specs=(
            P("dp", "tensor"),
            P("dp", "tensor"),
            P("tensor", "dp", None),
            P("tensor", "dp", None),
            P("tensor", "dp", None),
            P("tensor", "dp", None),
        ),
        check_vma=False,
    )
```

```python
import math

import jax
import jax.numpy as jnp
from jax import lax
from jax.experimental import pallas as pl
from jax.experimental.pallas import tpu as pltpu
from jax.sharding import PartitionSpec as P

BF16 = jnp.bfloat16
F32 = jnp.float32
NB, BS, HB = 64, 96, 256
POS = 6
LB = 4
FEAT = LB * BS
TOK = 2048
PIECES = 16
ALL_ROWS = 768
TILE = 1024
STEPS = TOK // TILE
WIDE = 1024
WIDE_STEPS = TOK // WIDE
ROOT_RATIO = math.sqrt(2.0 / math.pi)
DP_ORDER = (1, 8, 4, 2)
PARAMS = pltpu.CompilerParams(vmem_limit_bytes=63 * 1024 * 1024 + 512 * 1024)


def mm(lhs, rhs, left_dim=1, right_dim=0):
    return lax.dot_general(
        lhs, rhs, (((left_dim,), (right_dim,)), ((), ())), preferred_element_type=F32
    )


def whole(shape):
    return pl.BlockSpec(shape, lambda *_: (0,) * len(shape))


def columns(rows, tile=TILE):
    return pl.BlockSpec((rows, tile), lambda step: (0, step))


def token_rows():
    return pl.BlockSpec((WIDE, FEAT), lambda step: (step, 0))


def piece_rows(part):
    return pl.BlockSpec((PIECES, 48, 128), lambda *_: (0, part, 0))


def struct(shape, dtype=BF16):
    return jax.ShapeDtypeStruct(shape, dtype)


def cost(flops, moved):
    return pl.CostEstimate(flops=flops, bytes_accessed=moved, transcendentals=0)


def offset(place):
    return sum(((place >> level) & 1) * bit for level, bit in enumerate(DP_ORDER))


def pack_kernel(left_one_ref, left_two_ref, right_one_ref, right_two_ref, pieces_ref):
    left = [ref[row].astype(F32) for ref in (left_one_ref, left_two_ref) for row in range(6)]
    left = jnp.concatenate(left, axis=0)
    left = jnp.concatenate([left, jnp.zeros((48, 128 - BS), F32)], axis=1)
    two = [
        jnp.concatenate([right_two_ref[pos], right_two_ref[pos + POS // 2]], axis=1).astype(F32)
        for pos in range(POS // 2)
    ]
    one = [right_one_ref[pos].astype(F32) for pos in range(POS)]
    one = [rows[:, half : half + 128] for half in (0, 128) for rows in one]
    piece = jnp.concatenate([left] + two + one, axis=0).astype(BF16)
    for place in range(PIECES):
        pieces_ref[place] = piece


def pack(left_one, left_two, right_one, right_two):
    vmem = pl.BlockSpec(memory_space=pltpu.VMEM)
    return pl.pallas_call(
        pack_kernel,
        in_specs=[vmem] * 4,
        out_specs=vmem,
        out_shape=struct((PIECES, 144, 128)),
        compiler_params=PARAMS,
        cost_estimate=cost(1 << 20, 1 << 20),
        name="pack",
    )(left_one, left_two, right_one, right_two)


def prepare_kernel(
    perm_ref,
    visible_ref,
    patches_ref,
    tokens_ref,
    place_one_ref,
    place_two_ref,
    owner_ref,
    mix_ref,
    mask_ref,
    rep_ref,
    fold_ref,
    spread_ref,
):
    images, patch_count, _ = patches_ref.shape
    vis = visible_ref.shape[2]
    for image in range(images):
        wanted = visible_ref[image]
        chosen = lax.broadcasted_iota(jnp.int32, (patch_count, vis), 0) == wanted
        rows = mm(chosen.astype(F32).astype(BF16), patches_ref[image], 0, 0)
        tokens_ref[image * vis : (image + 1) * vis, :] = rows.astype(BF16)

    @pl.when(pl.program_id(0) == 0)
    def _():
        def tall(rows):
            return lax.broadcasted_iota(jnp.int32, (rows, 1), 0)

        def wide(cols):
            return lax.broadcasted_iota(jnp.int32, (1, cols), 1)

        def equal(left, right):
            return (left == right).astype(F32).astype(BF16)

        def parts(row, inner):
            outer = lax.div(row, inner)
            return outer, row - outer * inner

        def left_keys(row):
            piece, rest = parts(row, 48)
            which, rest = parts(rest, 24)
            near, block = parts(rest, LB)
            return which, piece * 6 + near, block

        which, source, block = left_keys(tall(ALL_ROWS))
        place_one_ref[...] = equal(jnp.where(which == 0, block * BS + source, -1), wide(FEAT))
        place_two_ref[...] = equal(jnp.where(which == 1, source * LB + block, -1), wide(FEAT))

        piece, rest = parts(tall(ALL_ROWS), 48)
        half, rest = parts(rest, 24)
        pos, near = parts(rest, 4)
        key = half * FEAT + pos * NB + piece * 4 + near
        owner_ref[...] = equal(key, wide(ALL_ROWS))

        piece, rest = parts(tall(FEAT), 24)
        pos, near = parts(rest, 4)
        blocks = jnp.concatenate([perm_ref[...]] * POS, axis=1)
        at, _ = parts(wide(FEAT), NB)
        mix_ref[...] = equal(pos * NB + piece * 4 + near, at * NB + blocks)

        outer, inner = parts(tall(FEAT), LB)
        block, within = parts(wide(FEAT), BS)
        mask_ref[...] = equal(inner, block)
        rep_ref[...] = equal(outer, wide(128))
        _, row_within = parts(tall(FEAT), BS)
        fold_ref[...] = equal(row_within, wide(128))
        spread_ref[...] = equal(tall(128), within)


def prepare(block_perm, visible, patches):
    images, patch_count, feats = patches.shape
    vis = visible.shape[1]
    group = 8
    shapes = [
        (ALL_ROWS, FEAT),
        (ALL_ROWS, FEAT),
        (ALL_ROWS, ALL_ROWS),
        (FEAT, FEAT),
        (FEAT, FEAT),
        (FEAT, 128),
        (FEAT, 128),
        (128, FEAT),
    ]
    return pl.pallas_call(
        prepare_kernel,
        grid=(images // group,),
        in_specs=[
            whole((1, NB)),
            pl.BlockSpec((group, 1, vis), lambda step: (step, 0, 0)),
            pl.BlockSpec((group, patch_count, feats), lambda step: (step, 0, 0)),
        ],
        out_specs=[pl.BlockSpec((group * vis, feats), lambda step: (step, 0))]
        + [whole(shape) for shape in shapes],
        out_shape=[struct((images * vis, feats))] + [struct(shape) for shape in shapes],
        compiler_params=PARAMS,
        cost_estimate=cost(2 * TOK * patch_count * feats, 12 << 20),
        name="prepare",
    )(block_perm[None, :], visible[:, None, :], patches)


def up_kernel(tokens_ref, pieces_ref, place_ref, rep_ref, mask_ref, matrix_ref, section_ref):
    @pl.when(pl.program_id(0) == 0)
    def _():
        pieces = pieces_ref[...].reshape(ALL_ROWS, 128)
        flat = mm(pieces, place_ref[...], 0, 0).astype(BF16)
        matrix_ref[...] = mm(rep_ref[...], flat).astype(BF16) * mask_ref[...]

    section_ref[...] = mm(matrix_ref[...], tokens_ref[...], 1, 1).astype(BF16)


def down_kernel(upstream_ref, pieces_ref, place_ref, spread_ref, mask_ref, matrix_ref, section_ref):
    @pl.when(pl.program_id(0) == 0)
    def _():
        pieces = pieces_ref[...].reshape(ALL_ROWS, 128)
        tall = mm(place_ref[...], pieces, 0, 0).astype(BF16)
        matrix_ref[...] = mm(tall, spread_ref[...]).astype(BF16) * mask_ref[...]

    section_ref[...] = mm(matrix_ref[...], upstream_ref[...], 1, 1).astype(BF16)


def block_map(kernel, name, rows, pieces, place, spread, mask):
    return pl.pallas_call(
        kernel,
        grid=(WIDE_STEPS,),
        in_specs=[
            token_rows(),
            piece_rows(0),
            whole(place.shape),
            whole(spread.shape),
            whole(mask.shape),
        ],
        out_specs=[whole((FEAT, FEAT)), columns(FEAT, WIDE)],
        out_shape=[struct((FEAT, FEAT)), struct((FEAT, TOK))],
        compiler_params=PARAMS,
        cost_estimate=cost(2 * TOK * FEAT * FEAT * 3, 5 << 20),
        name=name,
    )(rows, pieces, place, spread, mask)


def arrange_kernel(two_ref, one_ref, owner_ref, right_one_ref, right_two_ref):
    for pos in range(POS // 2):
        rows = two_ref[:, pos * 16 : pos * 16 + 16, :].reshape(HB, 128)
        right_two_ref[pos] = rows[:, :NB]
        right_two_ref[pos + POS // 2] = rows[:, NB:]
    both = mm(owner_ref[...], one_ref[...].reshape(ALL_ROWS, 128), 0, 0).astype(BF16)
    for pos in range(POS):
        right_one_ref[pos] = jnp.concatenate(
            [both[pos * NB : pos * NB + NB], both[FEAT + pos * NB : FEAT + pos * NB + NB]], axis=1
        )


def arrange(pieces, owner):
    return pl.pallas_call(
        arrange_kernel,
        grid=(1,),
        in_specs=[piece_rows(1), piece_rows(2), whole((ALL_ROWS, ALL_ROWS))],
        out_specs=[whole((POS, NB, HB)), whole((POS, HB, NB))],
        out_shape=[struct((POS, NB, HB)), struct((POS, HB, NB))],
        compiler_params=PARAMS,
        cost_estimate=cost(2 * ALL_ROWS * ALL_ROWS * 128, 3 << 20),
        name="arrange",
    )(pieces, pieces, owner)


def forward_kernel(
    arrived_ref, perm_ref, right_one_ref, right_two_ref, mixed_ref, act_ref, slope_ref, leaving_ref, own_ref
):
    mixed_ref[...] = mm(perm_ref[...], arrived_ref[...], 0, 0).astype(BF16)
    for pos in range(POS):
        rows = slice(pos * NB, (pos + 1) * NB)
        hidden_rows = slice(pos * HB, (pos + 1) * HB)
        hidden = mm(right_one_ref[pos], mixed_ref[rows, :], 0, 0)
        square = hidden * hidden
        tangent = jnp.tanh(hidden * (ROOT_RATIO + (ROOT_RATIO * 0.044715) * square))
        half = 0.5 * hidden
        act = (half + half * tangent).astype(BF16)
        slope = (0.5 + 0.5 * tangent) + half * (1.0 - tangent * tangent) * (
            ROOT_RATIO + (ROOT_RATIO * 3.0 * 0.044715) * square
        )
        act_ref[hidden_rows, :] = act
        slope_ref[hidden_rows, :] = slope.astype(BF16)
        own_ref[rows, :] = mm(right_two_ref[pos], act, 0, 0).astype(BF16)
    leaving_ref[...] = mm(perm_ref[...], own_ref[...]).astype(BF16)


def mix_forward(arrived, perm, right_one, right_two):
    return pl.pallas_call(
        forward_kernel,
        grid=(STEPS,),
        in_specs=[
            columns(FEAT),
            whole((FEAT, FEAT)),
            whole((POS, NB, HB)),
            whole((POS, HB, NB)),
        ],
        out_specs=[columns(FEAT), columns(POS * HB), columns(POS * HB), columns(FEAT)],
        out_shape=[
            struct((FEAT, TOK)),
            struct((POS * HB, TOK)),
            struct((POS * HB, TOK)),
            struct((FEAT, TOK)),
        ],
        scratch_shapes=[pltpu.VMEM((FEAT, TILE), BF16)],
        compiler_params=PARAMS,
        cost_estimate=cost(12 * TOK * FEAT * FEAT, 17 << 20),
        name="mix_forward",
    )(arrived, perm, right_one, right_two)


def backward_kernel(
    me_ref,
    arrived_ref,
    perm_ref,
    right_one_ref,
    right_two_ref,
    mixed_ref,
    act_ref,
    slope_ref,
    owner_ref,
    leaving_ref,
    kept_ref,
    sent_ref,
    grads_ref,
    own_ref,
    sum_one_ref,
    sum_two_ref,
    pair_ref,
    one_ref,
):
    step = pl.program_id(0)

    @pl.when(step == 0)
    def _():
        sum_one_ref[...] = jnp.zeros_like(sum_one_ref)
        sum_two_ref[...] = jnp.zeros_like(sum_two_ref)

    grads_ref[...] = mm(perm_ref[...], arrived_ref[...], 0, 0).astype(BF16)
    for pos in range(POS):
        rows = slice(pos * NB, (pos + 1) * NB)
        hidden_rows = slice(pos * HB, (pos + 1) * HB)
        grad_act = mm(right_two_ref[pos], grads_ref[rows, :])
        grad_hidden = (grad_act * slope_ref[hidden_rows, :].astype(F32)).astype(BF16)
        own_ref[rows, :] = mm(right_one_ref[pos], grad_hidden).astype(BF16)
        sum_one_ref[rows, :] += mm(mixed_ref[rows, :], grad_hidden, 1, 1)
        sum_two_ref[pos] += mm(act_ref[hidden_rows, :], grads_ref[rows, :], 1, 1)
    leaving_ref[...] = mm(perm_ref[...], own_ref[...]).astype(BF16)

    @pl.when(step == STEPS - 1)
    def _():
        me = me_ref[0]
        halves = jnp.concatenate([sum_one_ref[:, :128], sum_one_ref[:, 128:]], axis=0)
        one_ref[...] = mm(owner_ref[...], halves.astype(BF16)).astype(BF16)
        for pos in range(POS // 2):
            pair_ref[pos] = jnp.concatenate(
                [sum_two_ref[pos], sum_two_ref[pos + POS // 2]], axis=1
            )
        for piece in range(PIECES):
            of = me ^ offset(piece)
            start = pl.multiple_of(of * 16, 16)
            shares_ref = (kept_ref, sent_ref)[piece // 8]
            at = piece % 8 * 96
            for pos in range(POS // 2):
                shares_ref[at + pos * 16 : at + pos * 16 + 16, :] = pair_ref[
                    pos, pl.ds(start, 16), :
                ].astype(BF16)
            start = pl.multiple_of(of * 48, 16)
            shares_ref[at + 48 : at + 96, :] = one_ref[pl.ds(start, 48), :]


def mix_backward(me, arrived, perm, right_one, right_two, mixed, act, slope, owner):
    return pl.pallas_call(
        backward_kernel,
        grid=(STEPS,),
        in_specs=[
            pl.BlockSpec(memory_space=pltpu.SMEM),
            columns(FEAT),
            whole((FEAT, FEAT)),
            whole((POS, NB, HB)),
            whole((POS, HB, NB)),
            columns(FEAT),
            columns(POS * HB),
            columns(POS * HB),
            whole((ALL_ROWS, ALL_ROWS)),
        ],
        out_specs=[columns(FEAT), whole((ALL_ROWS, 128)), whole((ALL_ROWS, 128))],
        out_shape=[struct((FEAT, TOK)), struct((ALL_ROWS, 128)), struct((ALL_ROWS, 128))],
        scratch_shapes=[
            pltpu.VMEM((FEAT, TILE), BF16),
            pltpu.VMEM((FEAT, TILE), BF16),
            pltpu.VMEM((FEAT, HB), F32),
            pltpu.VMEM((POS, HB, NB), F32),
            pltpu.VMEM((POS // 2, HB, 2 * NB), F32),
            pltpu.VMEM((ALL_ROWS, 128), BF16),
        ],
        compiler_params=PARAMS,
        cost_estimate=cost(20 * TOK * FEAT * FEAT, 17 << 20),
        name="mix_backward",
    )(me, arrived, perm, right_one, right_two, mixed, act, slope, owner)


def second_grad_kernel(
    returned_ref, upstream_ref, mask_ref, fold_ref, order_ref, shares_ref, sum_ref
):
    step = pl.program_id(0)

    @pl.when(step == 0)
    def _():
        sum_ref[...] = jnp.zeros_like(sum_ref)

    sum_ref[...] += mm(returned_ref[...], upstream_ref[...])

    @pl.when(step == WIDE_STEPS - 1)
    def _():
        kept = sum_ref[...].astype(BF16) * mask_ref[...]
        flat = mm(kept, fold_ref[...]).astype(BF16)
        shares_ref[...] = mm(order_ref[...], flat).astype(BF16)


def second_grad(returned, upstream, mask, fold, order):
    return pl.pallas_call(
        second_grad_kernel,
        grid=(WIDE_STEPS,),
        in_specs=[
            columns(FEAT, WIDE),
            token_rows(),
            whole((FEAT, FEAT)),
            whole((FEAT, 128)),
            whole((ALL_ROWS, FEAT)),
        ],
        out_specs=whole((ALL_ROWS, 128)),
        out_shape=struct((ALL_ROWS, 128)),
        scratch_shapes=[pltpu.VMEM((FEAT, FEAT), F32)],
        compiler_params=PARAMS,
        cost_estimate=cost(2 * TOK * FEAT * FEAT, 4 << 20),
        name="second_grad",
    )(returned, upstream, mask, fold, order)


def first_grad_kernel(
    returned_ref,
    tokens_ref,
    mask_ref,
    rep_ref,
    order_ref,
    second_ref,
    shares_ref,
    sum_ref,
):
    step = pl.program_id(0)

    @pl.when(step == 0)
    def _():
        sum_ref[...] = jnp.zeros_like(sum_ref)

    sum_ref[...] += mm(returned_ref[...], tokens_ref[...])

    @pl.when(step == WIDE_STEPS - 1)
    def _():
        kept = sum_ref[...].astype(BF16) * mask_ref[...]
        flat = mm(rep_ref[...], kept, 0, 0).astype(BF16)
        shares_ref[...] = (mm(order_ref[...], flat, 1, 1) + second_ref[...].astype(F32)).astype(BF16)


def first_grad(returned, tokens, mask, rep, order, second):
    return pl.pallas_call(
        first_grad_kernel,
        grid=(WIDE_STEPS,),
        in_specs=[
            columns(FEAT, WIDE),
            token_rows(),
            whole((FEAT, FEAT)),
            whole((FEAT, 128)),
            whole((ALL_ROWS, FEAT)),
            whole((ALL_ROWS, 128)),
        ],
        out_specs=whole((ALL_ROWS, 128)),
        out_shape=struct((ALL_ROWS, 128)),
        scratch_shapes=[pltpu.VMEM((FEAT, FEAT), F32)],
        compiler_params=PARAMS,
        cost_estimate=cost(2 * TOK * FEAT * FEAT, 3 << 20),
        name="first_grad",
    )(returned, tokens, mask, rep, order, second)


def outputs_kernel(returned_ref, matrix_two_ref, returned_grad_ref, matrix_one_ref, out_ref, grad_ref):
    out_ref[...] = mm(returned_ref[...], matrix_two_ref[...], 0, 0).astype(BF16)
    grad_ref[...] = mm(returned_grad_ref[...], matrix_one_ref[...], 0, 0).astype(BF16)


def outputs(returned, matrix_two, returned_grad, matrix_one):
    return pl.pallas_call(
        outputs_kernel,
        grid=(WIDE_STEPS,),
        in_specs=[
            columns(FEAT, WIDE),
            whole((FEAT, FEAT)),
            columns(FEAT, WIDE),
            whole((FEAT, FEAT)),
        ],
        out_specs=[token_rows(), token_rows()],
        out_shape=[struct((TOK, FEAT)), struct((TOK, FEAT))],
        compiler_params=PARAMS,
        cost_estimate=cost(4 * TOK * FEAT * FEAT, 7 << 20),
        name="outputs",
    )(returned, matrix_two, returned_grad, matrix_one)


def exchange(x, bit):
    return lax.ppermute(x, "dp", [(i, i ^ bit) for i in range(PIECES)])


def added(one, other):
    return (one.astype(F32) + other.astype(F32)).astype(BF16)


def halved(x, bit):
    rows = x.shape[0] // 2
    return added(x[:rows], exchange(x[rows:], bit))


def to_tensor(x):
    return lax.all_to_all(x, "tensor", split_axis=0, concat_axis=0, tiled=True)


def local(
    patches, visible, block_perm, first_left, first_right, second_right, second_left, cotangent
):
    tie = lax.optimization_barrier
    me = lax.axis_index("dp").astype(jnp.int32).reshape(1)

    pieces = pack(
        first_left.transpose(1, 0, 2), second_left.transpose(1, 0, 2), first_right, second_right
    )
    pieces = lax.all_to_all(pieces, "dp", split_axis=0, concat_axis=0, tiled=True)

    tokens, place_one, place_two, owner, perm, mask, rep, fold, spread = prepare(
        block_perm, visible, patches
    )
    pieces, tokens = tie((pieces, tokens))

    matrix_one, section_one = block_map(
        up_kernel, "first_map", tokens, pieces, place_one, rep, mask
    )
    arrived = to_tensor(section_one)
    matrix_two, back_grad = block_map(
        down_kernel, "second_map_back", cotangent, pieces, place_two, spread, mask
    )
    right_one, right_two = arrange(pieces, owner)
    arrived, back_grad, right_one = tie((arrived, back_grad, right_one))
    arrived_grad = to_tensor(back_grad)

    mixed, act, slope, leaving = mix_forward(arrived, perm, right_one, right_two)
    leaving, arrived_grad = tie((leaving, arrived_grad))
    returned = to_tensor(leaving)
    leaving_grad, kept, sent = mix_backward(
        me, arrived_grad, perm, right_one, right_two, mixed, act, slope, owner
    )
    right_shares = added(kept, exchange(sent, DP_ORDER[3]))
    returned, leaving_grad, right_shares = tie((returned, leaving_grad, right_shares))
    returned_grad = to_tensor(leaving_grad)
    grad_left_two = second_grad(returned, cotangent, mask, fold, place_two)
    right_shares, grad_left_two = tie((right_shares, grad_left_two))
    right_shares = halved(right_shares, DP_ORDER[2])
    right_shares = halved(right_shares, DP_ORDER[1])

    left_held = first_grad(
        returned_grad, tokens, mask, rep, place_one, grad_left_two
    )
    left_shares = lax.all_to_all(left_held, "dp", split_axis=0, concat_axis=0, tiled=True)
    returned_grad, right_shares, left_held = tie((returned_grad, right_shares, left_held))
    output, token_grad = outputs(returned, matrix_two, returned_grad, matrix_one)

    right_total = halved(right_shares, DP_ORDER[0]).astype(F32)

    left_total = jnp.sum(left_shares.reshape(PIECES, 48, 128).astype(F32), axis=0)[:, :BS]
    left_total = left_total.reshape(2, 6, LB, BS).transpose(0, 2, 1, 3)
    two_total = right_total[:48].reshape(3, 16, 2, NB).transpose(2, 0, 1, 3).reshape(POS, 16, NB)
    one_total = jnp.concatenate([right_total[48:72], right_total[72:]], axis=1)
    one_total = one_total.reshape(POS, 4, HB)
    return (output, token_grad, left_total[0], one_total, two_total, left_total[1])


def solution(mesh):
    placed = (
        P("dp", None, "tensor"),
        P("dp", None),
        P(),
        P("tensor", "dp", None),
        P("tensor", "dp", None),
        P("tensor", "dp", None),
        P("tensor", "dp", None),
        P("dp", "tensor"),
    )
    return jax.shard_map(
        local,
        mesh=mesh,
        in_specs=placed,
        out_specs=(
            P("dp", "tensor"),
            P("dp", "tensor"),
            P("tensor", "dp", None),
            P("tensor", "dp", None),
            P("tensor", "dp", None),
            P("tensor", "dp", None),
        ),
        check_vma=False,
    )
```
